32 devices in a mesh: shots: 2 (over x), lat: 16 (over z, y, core).
Axes of the slice: x: 2, y: 2, z: 4, core: 2. Of those that a mesh axis runs over, the one named last changes fastest.
Arguments:
- source_field: float32 [4, 2, 1024, 1024], P('shots', None, 'lat'), parts along dimension 0, may hold values from -6 to 6
- receiver_field: float32 [4, 2, 1024, 1024], P('shots', None, 'lat'), parts along dimension 0, may hold values from -6 to 6
- ref_slowness: float32 [2], replicated, may hold values from 0.6 to 1.3
- omega: float32 [2], replicated, may hold values from 1 to 2.5
- interp_index: int32 [1024, 1024], P('lat'), may hold values from 0 to 7
- lags: int32 [16], replicated, may hold values from -16 to 16, as said below
Outputs:
- images: float32 [32, 1024, 1024], P('shots', 'lat'), parts along dimension 0
The draws below stay inside these ranges and needn't reach their ends.
There are 2 independent parts, one for each index of `shots`. The reference program is written for one: setup_inputs(seed, part) draws one part's arguments, and reference() takes and returns one part's arrays. A program takes and returns all parts, laid end to end along the dimension named above; an argument that names none is the same for every part. Nothing has to cross between parts.
Inputs may be any that keep to these rules, and one draw needn't show every extreme that they name: `lags`: offsets lie in -16 to 16, and both ends occur.
All inputs are finite; a program needn't handle non-finite values.
Results may differ from the reference program's by a relative error of at most 0.0003.
Values sent between devices are 32-bit elements; how exact they have to be, the bound alone decides.
A program may use at most 128 MiB of HBM per device.

```python
import math
import jax
import jax.numpy as jnp
from jax import lax

NX = 1024
NY = 1024
FREQ = 2
HMAX = 16
NLAG = 16
INTERP = 8


def draw_lags(key, part):
    key = jax.random.fold_in(key, 7)
    others = jax.random.randint(key, (NLAG - 2,), -HMAX, HMAX + 1).astype(jnp.int32)
    ends = jnp.array([-HMAX, HMAX], dtype=jnp.int32)
    return jnp.concatenate([ends, others])


def set_ends(values, rng, low, high):
    longest = values.shape.index(max(values.shape))
    spots = []
    for shift in (0, 1):
        where = [jax.random.randint(jax.random.fold_in(rng, axis), (), 0, length) for axis, length in enumerate(values.shape)]
        where[longest] = (where[longest] + shift) % values.shape[longest]
        spots.append(tuple(where))
    return values.at[spots[0]].set(low).at[spots[1]].set(high)


def levels(rng, dims, cuts, smallest, largest):
    level = 1.0
    for dim, blocks in cuts:
        heights = jax.random.uniform(jax.random.fold_in(jax.random.fold_in(rng, 6), dim), (blocks,), jnp.float32, smallest / len(cuts), largest / len(cuts))
        level = level * jnp.repeat(jnp.exp(heights), dims[dim] // blocks).reshape((-1,) + (1,) * (len(dims) - 1 - dim))
    return level


def scatter_about(own_key, shape, width, most, split=(), held_as=jnp.bfloat16):
    gain = levels(own_key, shape, split, -0.22, 0.18) if split else 1.0
    drawn = jax.random.normal(own_key, shape, jnp.float32) * width * gain
    return jnp.minimum(jnp.maximum(drawn, -most), most).astype(held_as)


def setup_inputs(seed: int = 0, part: int = 0) -> dict:
    keys = jax.random.split(jax.random.key(seed), 7)
    own_keys = jax.random.split(jax.random.fold_in(keys[6], part), 7)
    source_field = scatter_about(own_keys[0], (FREQ, 2, NX, NY), 1.0, 6.0, ((2, 16),), jnp.float32)
    receiver_field = scatter_about(own_keys[1], (FREQ, 2, NX, NY), 1.0, 6.0, ((2, 16),), jnp.float32)
    ref_slowness = jnp.clip(jnp.exp(jax.random.uniform(keys[2], (2,), jnp.float32, math.log(0.6), math.log(1.3))), 0.6, 1.3)
    omega = jnp.clip(jax.random.uniform(keys[3], (FREQ,), jnp.float32, 1.0, 2.5), 1.0, 2.5)
    interp_index = set_ends(jax.random.randint(keys[4], (NX, NY), 0, INTERP), jax.random.fold_in(keys[4], 1), 0, INTERP - 1).astype(jnp.int32)
    lags = draw_lags(jax.random.fold_in(keys[6], 71), part)
    return dict(source_field=source_field, receiver_field=receiver_field, ref_slowness=ref_slowness, omega=omega, interp_index=interp_index, lags=lags)


depth_step = 2.0

def wave_numbers(count):
    index = jnp.arange(count, dtype=jnp.int32)
    signed = jnp.where(index < count // 2, index, index - count)
    return signed.astype(jnp.float32) * (2.0 * math.pi / count)

def reference(source_field, receiver_field, ref_slowness, omega, interp_index, lags):
    kx = wave_numbers(NX)
    ky = wave_numbers(NY)
    lateral = kx[:, None] ** 2 + ky[None, :] ** 2
    weight = interp_index.astype(jnp.float32) / (INTERP - 1)

    def migrate(field, sign):
        wave = field[:, 0] + 1j * field[:, 1]
        spectrum = jnp.fft.fft2(wave, axes=(1, 2))
        results = []
        for j in range(2):
            vertical = (omega * ref_slowness[j]) ** 2
            arg = vertical[:, None, None] - lateral[None]
            phase = jnp.sqrt(jnp.maximum(arg, 0.0)) * depth_step
            decay = jnp.exp(-jnp.sqrt(jnp.maximum(-arg, 0.0)) * depth_step)
            shift = decay * (jnp.cos(phase) + 1j * sign * jnp.sin(phase))
            results.append(jnp.fft.ifft2(spectrum * shift, axes=(1, 2)))
        mixed = (1.0 - weight) * results[0] + weight * results[1]
        return (jnp.real(mixed), jnp.imag(mixed))
    src_real, src_imag = migrate(source_field, -1.0)
    rec_real, rec_imag = migrate(receiver_field, 1.0)
    widths = ((0, 0), (HMAX, HMAX), (0, 0))
    src_real = jnp.pad(src_real, widths)
    src_imag = jnp.pad(src_imag, widths)
    rec_real = jnp.pad(rec_real, widths)
    rec_imag = jnp.pad(rec_imag, widths)

    def one_offset(lag):
        low = (HMAX - lag).astype(jnp.int32)
        high = (HMAX + lag).astype(jnp.int32)
        s_real = lax.dynamic_slice_in_dim(src_real, low, NX, 1)
        s_imag = lax.dynamic_slice_in_dim(src_imag, low, NX, 1)
        r_real = lax.dynamic_slice_in_dim(rec_real, high, NX, 1)
        r_imag = lax.dynamic_slice_in_dim(rec_imag, high, NX, 1)
        return lax.optimization_barrier(jnp.sum(s_real * r_real + s_imag * r_imag, axis=0))
    return lax.map(one_offset, lags)
```

```python
import functools
import math

import jax
import jax.numpy as jnp
import ml_dtypes
import numpy as np
from jax import lax
from jax.experimental import pallas as pl
from jax.experimental.pallas import tpu as pltpu
from jax.sharding import PartitionSpec as P

HMAX = 16
INTERP = 8


depth_step = 2.0
highest = lax.Precision.HIGHEST


def extended(block, sides, width):
    for axis, dim in sides:
        count = lax.axis_size(axis)
        forward = [(i, i + 1) for i in range(count - 1)]
        backward = [(target, source) for source, target in forward]
        low = lax.ppermute(
            lax.slice_in_dim(block, block.shape[dim] - width, None, axis=dim), axis, forward
        )
        high = lax.ppermute(lax.slice_in_dim(block, 0, width, axis=dim), axis, backward)
        block = jnp.concatenate([low, block, high], axis=dim)
    return block


def dft_tables(count):
    index = jnp.arange(count, dtype=jnp.int32)
    turns = index[:, None] * index[None, :] % count
    angle = turns.astype(jnp.float32) * (2.0 * math.pi / count)
    return (jnp.cos(angle), jnp.sin(angle))


def wave_numbers(count):
    index = jnp.arange(count, dtype=jnp.int32)
    signed = jnp.where(index < count // 2, index, index - count)
    return signed.astype(jnp.float32) * (2.0 * math.pi / count)


def factor_pair(count):
    first = 1
    for divisor in range(1, int(math.isqrt(count)) + 1):
        if count % divisor == 0:
            first = divisor
    return (first, count // first)


def complex_apply(real_part, imag_part, cosine, sine, form, sign):
    stacked = jnp.stack([real_part, imag_part], axis=0)
    with_cos = jnp.einsum(form, stacked, cosine, precision=highest)
    with_sin = jnp.einsum(form, stacked, sine, precision=highest)
    return (with_cos[0] - sign * with_sin[1], with_cos[1] + sign * with_sin[0])


def dft_axis(real_part, imag_part, axis, sign, factor):
    count = real_part.shape[axis]
    first, second = factor_pair(count)
    real_part = jnp.moveaxis(real_part, axis, -1)
    imag_part = jnp.moveaxis(imag_part, axis, -1)
    leading = real_part.shape[:-1]
    real_part = real_part.reshape(leading + (first, second))
    imag_part = imag_part.reshape(leading + (first, second))
    cos_a, sin_a = dft_tables(first)
    real_part, imag_part = complex_apply(
        real_part, imag_part, cos_a, sin_a, "...ab,ac->...cb", sign
    )
    row_index = jnp.arange(first, dtype=jnp.int32)[:, None]
    col_index = jnp.arange(second, dtype=jnp.int32)[None, :]
    twist = (row_index * col_index % count).astype(jnp.float32) * (2.0 * math.pi / count)
    cos_t = jnp.cos(twist)
    sin_t = sign * jnp.sin(twist)
    real_part, imag_part = (
        real_part * cos_t - imag_part * sin_t,
        real_part * sin_t + imag_part * cos_t,
    )
    cos_b, sin_b = dft_tables(second)
    real_part, imag_part = complex_apply(
        real_part, imag_part, cos_b, sin_b, "...cb,bd->...cd", sign
    )
    real_part = jnp.swapaxes(real_part, -1, -2).reshape(leading + (count,)) * factor
    imag_part = jnp.swapaxes(imag_part, -1, -2).reshape(leading + (count,)) * factor
    return (jnp.moveaxis(real_part, -1, axis), jnp.moveaxis(imag_part, -1, axis))


def send_out_each(spectrum):
    return lax.all_to_all(spectrum, "lat", split_axis=4, concat_axis=3, tiled=True)


def send_back_each(fields):
    return lax.all_to_all(fields, "lat", split_axis=4, concat_axis=5, tiled=True)


def propagate(fields, omegas, ref_slowness, send_out, send_back):
    n_y = fields.shape[4]
    n_x = fields.shape[3] * lax.axis_size("lat")
    real_part, imag_part = dft_axis(fields[:, :, 0], fields[:, :, 1], 3, -1.0, 1.0)
    turned = send_out(jnp.stack([real_part, imag_part], axis=2))
    n_cols = turned.shape[4]
    real_part, imag_part = dft_axis(turned[:, :, 0], turned[:, :, 1], 2, -1.0, 1.0)
    real_part = jnp.swapaxes(real_part, 2, 3)
    imag_part = jnp.swapaxes(imag_part, 2, 3)
    ky_all = wave_numbers(n_y)
    ky = lax.dynamic_slice_in_dim(ky_all, lax.axis_index("lat") * n_cols, n_cols)
    kx = wave_numbers(n_x)
    lateral = ky[:, None] ** 2 + kx[None, :] ** 2
    direction = jnp.array([-1.0, 1.0], dtype=jnp.float32)[:, None, None, None]
    shifted = []
    for j in range(2):
        vertical = (omegas * ref_slowness[j]) ** 2
        arg = vertical[:, None, None] - lateral[None]
        phase = jnp.sqrt(jnp.maximum(arg, 0.0)) * depth_step
        decay = jnp.exp(-jnp.sqrt(jnp.maximum(-arg, 0.0)) * depth_step)
        cos_shift = (decay * jnp.cos(phase))[None]
        sin_shift = direction * (decay * jnp.sin(phase))[None]
        new_real = real_part * cos_shift - imag_part * sin_shift
        new_imag = real_part * sin_shift + imag_part * cos_shift
        back_real, back_imag = dft_axis(new_real, new_imag, 3, 1.0, 1.0 / n_x)
        back_real = jnp.swapaxes(back_real, 2, 3)
        back_imag = jnp.swapaxes(back_imag, 2, 3)
        shifted.append(jnp.stack([back_real, back_imag], axis=2))
    returned = send_back(jnp.stack(shifted, axis=0))
    out_real, out_imag = dft_axis(returned[:, :, :, 0], returned[:, :, :, 1], 4, 1.0, 1.0 / n_y)
    return jnp.stack([out_real, out_imag], axis=3)


def local(source_field, receiver_field, ref_slowness, omega, interp_index, lags):
    fields = jnp.stack([source_field, receiver_field], axis=0)
    pieces = []
    for step in range(fields.shape[1]):
        pieces.append(
            propagate(
                fields[:, step : step + 1],
                omega[step : step + 1],
                ref_slowness,
                send_out_each,
                send_back_each,
            )
        )
    references = jnp.concatenate(pieces, axis=2)
    weight = interp_index.astype(jnp.float32) / (INTERP - 1)
    migrated = (1.0 - weight) * references[0] + weight * references[1]
    padded = extended(migrated, (("lat", 3),), HMAX)
    rows = migrated.shape[3]

    def one_offset(lag):
        source_rows = lax.dynamic_slice_in_dim(padded[0], HMAX - lag, rows, 2)
        receiver_rows = lax.dynamic_slice_in_dim(padded[1], HMAX + lag, rows, 2)
        return jnp.sum(source_rows * receiver_rows, axis=(0, 1))

    return lax.map(one_offset, lags)


RADIX = 4
SUB = 256
POINTS = RADIX * SUB
PEERS = 16
ROWS = POINTS // PEERS
LANES = 2 * ROWS
BANDS = POINTS // LANES
MESH = pl.DeviceIdType.MESH


def fourier_tables():
    r = np.arange(RADIX)[:, None, None]
    m = np.arange(SUB)[None, :, None]
    y = np.arange(SUB)[None, None, :]
    angle = ((r + RADIX * m) * y % POINTS) * (2.0 * np.pi / POINTS)
    both = np.stack([np.cos(angle), np.sin(angle)], axis=1).astype(np.float32)
    high = both.astype(ml_dtypes.bfloat16)
    low = (both - high.astype(np.float32)).astype(ml_dtypes.bfloat16)
    straight = np.stack([high, low], axis=2)
    return np.stack([straight, np.swapaxes(straight, -1, -2)])


def split(value):
    high = value.astype(jnp.bfloat16)
    low = (value - high.astype(jnp.float32)).astype(jnp.bfloat16)
    return high, low


def dot(a, b):
    return jnp.dot(a, b, preferred_element_type=jnp.float32)


def table_left(tab_ref, turned, r, trig, pair):
    high, low = tab_ref[turned, r, trig, 0], tab_ref[turned, r, trig, 1]
    return dot(high, pair[0]) + (dot(high, pair[1]) + dot(low, pair[0]))


def table_right(tab_ref, turned, r, trig, pair):
    high, low = tab_ref[turned, r, trig, 0], tab_ref[turned, r, trig, 1]
    return dot(pair[0], high) + (dot(pair[1], high) + dot(pair[0], low))


def forward_four(re, im):
    pr, mr, qr, nr = re[0] + re[2], re[0] - re[2], re[1] + re[3], re[1] - re[3]
    pi, mi, qi, ni = im[0] + im[2], im[0] - im[2], im[1] + im[3], im[1] - im[3]
    return (
        [pr + qr, mr + ni, pr - qr, mr - ni],
        [pi + qi, mi - nr, pi - qi, mi + nr],
    )


def backward_four(re, im):
    pr, mr, qr, nr = re[0] + re[2], re[0] - re[2], re[1] + re[3], re[1] - re[3]
    pi, mi, qi, ni = im[0] + im[2], im[0] - im[2], im[1] + im[3], im[1] - im[3]
    return (
        [pr + qr, mr - ni, pr - qr, mr + ni],
        [pi + qi, mi + nr, pi - qi, mi - nr],
    )


def signed_wave(index):
    signed = jnp.where(index < POINTS // 2, index, index - POINTS)
    return signed.astype(jnp.float32) * (2.0 * math.pi / POINTS)


def series(square, terms):
    total = jnp.full_like(square, terms[-1])
    for term in terms[-2::-1]:
        total = total * square + term
    return total


SIN_TERMS = [(-1.0) ** i / math.factorial(2 * i + 1) for i in range(8)]
COS_TERMS = [(-1.0) ** i / math.factorial(2 * i) for i in range(8)]


def shift_pair(arg):
    root = jnp.sqrt(jnp.abs(arg))
    half = root - 0.5 * math.pi
    square = half * half
    sine = half * series(square, SIN_TERMS)
    cosine = series(square, COS_TERMS)
    moving = arg > 0.0
    decay = jnp.exp(-depth_step * root)
    real = jnp.where(moving, 2.0 * sine * sine - 1.0, decay)
    imag = jnp.where(moving, -2.0 * sine * cosine, 0.0)
    return real, imag


def halves(first, second, low_half):
    low = jnp.where(low_half, first, pltpu.roll(second, ROWS, 1))
    high = jnp.where(low_half, pltpu.roll(first, ROWS, 1), second)
    return low, high


def migrate_kernel(
    omega_ref, slow_ref, src_ref, rec_ref, index_ref, tab_ref, out_ref,
    send_f, recv_f, send_b, recv_b, spec, shift, first_ref,
    sem_fs, sem_fr, sem_bs, sem_br, sem_hs, sem_hr,
):
    me = lax.axis_index("lat")
    n = PEERS
    lane = lax.broadcasted_iota(jnp.int32, (ROWS, LANES), 1)
    low_half = lane < ROWS

    def copy_f(w, d):
        to = lax.rem(me + d, n)
        return pltpu.make_async_remote_copy(
            src_ref=send_f.at[w, to], dst_ref=recv_f.at[w, me],
            send_sem=sem_fs.at[w, d], recv_sem=sem_fr.at[w, d],
            device_id={"lat": to}, device_id_type=MESH,
        )

    def copy_b(w, j, d):
        to = lax.rem(me + d, n)
        return pltpu.make_async_remote_copy(
            src_ref=send_b.at[w, j, to], dst_ref=recv_b.at[w, j, me],
            send_sem=sem_bs.at[w, j, d], recv_sem=sem_br.at[w, j, d],
            device_id={"lat": to}, device_id_type=MESH,
        )

    def got_f(w, d):
        origin = lax.rem(me + n - d, n)
        return pltpu.make_async_remote_copy(
            src_ref=send_f.at[w, me], dst_ref=recv_f.at[w, origin],
            send_sem=sem_fs.at[w, d], recv_sem=sem_fr.at[w, d],
            device_id={"lat": origin}, device_id_type=MESH,
        )

    def got_b(w, j, d):
        origin = lax.rem(me + n - d, n)
        return pltpu.make_async_remote_copy(
            src_ref=send_b.at[w, j, me], dst_ref=recv_b.at[w, j, origin],
            send_sem=sem_bs.at[w, j, d], recv_sem=sem_br.at[w, j, d],
            device_id={"lat": origin}, device_id_type=MESH,
        )

    def halo(w, side):
        to, take, put = (me + 1, ROWS, 0) if side == 0 else (me - 1, HMAX, HMAX + ROWS)
        return pltpu.make_async_remote_copy(
            src_ref=out_ref.at[w, :, :, :, pl.ds(take, HMAX), :],
            dst_ref=out_ref.at[w, :, :, :, pl.ds(put, HMAX), :],
            send_sem=sem_hs.at[w, side], recv_sem=sem_hr.at[w, side],
            device_id={"lat": to}, device_id_type=MESH,
        )

    def every(body):
        @pl.loop(1, n)
        def _(d):
            body(d)

    barrier = pltpu.get_barrier_semaphore()

    def greet(d):
        pl.semaphore_signal(
            barrier, inc=1, device_id={"lat": lax.rem(me + d, n)}, device_id_type=MESH
        )

    every(greet)

    def rows_forward(w):
        re, im = [], []
        for q in range(RADIX):
            cut = pl.ds(q * SUB, SUB)
            re.append(jnp.concatenate([src_ref[w, 0, :, cut], rec_ref[w, 0, :, cut]], axis=0))
            im.append(jnp.concatenate([src_ref[w, 1, :, cut], rec_ref[w, 1, :, cut]], axis=0))
        re, im = forward_four(re, im)
        for r in range(RADIX):
            pair = split(jnp.concatenate([re[r], im[r]], axis=0))
            with_cos = table_right(tab_ref, 1, r, 0, pair)
            with_sin = table_right(tab_ref, 1, r, 1, pair)
            parts = (
                with_cos[:LANES] + with_sin[LANES:],
                with_cos[LANES:] - with_sin[:LANES],
            )
            for c in range(2):
                for b in range(2):
                    piece = parts[c][:, b * LANES : (b + 1) * LANES]
                    low, high = halves(piece[:ROWS], piece[ROWS:], low_half)
                    peer = RADIX * r + 2 * b
                    send_f[w, peer, c] = low
                    send_f[w, peer + 1, c] = high

    def make_shift(w, j):
        speed = omega_ref[w] * slow_ref[j]
        vertical = speed * speed
        wide = lax.broadcasted_iota(jnp.int32, (ROWS, LANES), 1)
        tall = lax.broadcasted_iota(jnp.int32, (ROWS, LANES), 0)
        place = ROWS * me + lax.rem(wide, ROWS)
        ky = signed_wave(place // SUB + RADIX * lax.rem(place, SUB))
        ky2 = ky * ky
        sign = jnp.where(wide < ROWS, -1.0, 1.0)
        scale = 1.0 / (POINTS * POINTS)

        @pl.loop(0, PEERS)
        def _(block):
            at = ROWS * block
            r = at // SUB
            kx = signed_wave(r + RADIX * (lax.rem(at, SUB) + tall))
            real, imag = shift_pair(vertical - (kx * kx + ky2))
            rows = pl.ds(pl.multiple_of(ROWS * block, ROWS), ROWS)
            shift[w, j, 0, rows, :] = real * scale
            shift[w, j, 1, rows, :] = imag * (sign * scale)

    def columns_forward(w):
        re, im = [], []
        for q in range(RADIX):
            re.append(recv_f[w, 4 * q : 4 * q + 4, 0].reshape(SUB, LANES))
            im.append(recv_f[w, 4 * q : 4 * q + 4, 1].reshape(SUB, LANES))
        re, im = forward_four(re, im)
        for r in range(RADIX):
            pair = split(jnp.concatenate([re[r], im[r]], axis=1))
            with_cos = table_left(tab_ref, 0, r, 0, pair)
            with_sin = table_left(tab_ref, 0, r, 1, pair)
            spec[r, 0] = with_cos[:, :LANES] + with_sin[:, LANES:]
            spec[r, 1] = with_cos[:, LANES:] - with_sin[:, :LANES]

    def columns_backward(w, j):
        re, im = [], []
        for r in range(RADIX):
            cos_shift = shift[w, j, 0, pl.ds(r * SUB, SUB), :]
            sin_shift = shift[w, j, 1, pl.ds(r * SUB, SUB), :]
            new_re = spec[r, 0] * cos_shift - spec[r, 1] * sin_shift
            new_im = spec[r, 0] * sin_shift + spec[r, 1] * cos_shift
            pair = split(jnp.concatenate([new_re, new_im], axis=1))
            with_cos = table_left(tab_ref, 1, r, 0, pair)
            with_sin = table_left(tab_ref, 1, r, 1, pair)
            re.append(with_cos[:, :LANES] - with_sin[:, LANES:])
            im.append(with_cos[:, LANES:] + with_sin[:, :LANES])
        re, im = backward_four(re, im)
        for q in range(RADIX):
            send_b[w, j, 4 * q : 4 * q + 4, 0] = re[q].reshape(4, ROWS, LANES)
            send_b[w, j, 4 * q : 4 * q + 4, 1] = im[q].reshape(4, ROWS, LANES)

    def rows_backward(w, j):
        re, im = [], []
        for r in range(RADIX):
            stacked = []
            for c in range(2):
                sides = [
                    halves(recv_b[w, j, 4 * r + 2 * b, c], recv_b[w, j, 4 * r + 2 * b + 1, c], low_half)
                    for b in range(2)
                ]
                for field in range(2):
                    stacked.append(jnp.concatenate([sides[0][field], sides[1][field]], axis=1))
            pair = split(jnp.concatenate(stacked, axis=0))
            with_cos = table_right(tab_ref, 0, r, 0, pair)
            with_sin = table_right(tab_ref, 0, r, 1, pair)
            re.append(with_cos[:LANES] - with_sin[LANES:])
            im.append(with_cos[LANES:] + with_sin[:LANES])
        parts = backward_four(re, im)
        for q in range(RADIX):
            cut = pl.ds(q * SUB, SUB)
            weight = index_ref[:, cut].astype(jnp.float32) / (INTERP - 1)
            for c in range(2):
                for field in range(2):
                    value = parts[c][q][ROWS * field : ROWS * (field + 1)]
                    if j == 0:
                        first_ref[field, c, :, cut] = (1.0 - weight) * value
                    else:
                        mixed = first_ref[field, c, :, cut] + weight * value
                        for b in range(2):
                            out_ref[w, field, c, 2 * q + b, pl.ds(HMAX, ROWS), :] = (
                                mixed[:, b * LANES : (b + 1) * LANES]
                            )

    @pl.when(me == 0)
    def _():
        for w in range(2):
            out_ref[w, :, :, :, pl.ds(0, HMAX), :] = jnp.zeros((2, 2, BANDS, HMAX, LANES), jnp.float32)

    @pl.when(me == n - 1)
    def _():
        for w in range(2):
            out_ref[w, :, :, :, pl.ds(HMAX + ROWS, HMAX), :] = jnp.zeros((2, 2, BANDS, HMAX, LANES), jnp.float32)

    rows_forward(0)
    pl.semaphore_wait(barrier, n - 1)
    every(lambda d: copy_f(0, d).start())
    rows_forward(1)
    every(lambda d: copy_f(1, d).start())
    for w in range(2):
        recv_f[w, me] = send_f[w, me]
        for j in range(2):
            make_shift(w, j)
    for w in range(2):
        every(lambda d: got_f(w, d).wait_recv())
        columns_forward(w)
        for j in range(2):
            columns_backward(w, j)
            every(lambda d: copy_b(w, j, d).start())
            recv_b[w, j, me] = send_b[w, j, me]
    for w in range(2):
        for j in range(2):
            every(lambda d: got_b(w, j, d).wait_recv())
            rows_backward(w, j)

        @pl.when(me < n - 1)
        def _():
            halo(w, 0).start()

        @pl.when(me > 0)
        def _():
            halo(w, 1).start()

    for w in range(2):
        every(lambda d: copy_f(w, d).wait_send())
        for j in range(2):
            every(lambda d: copy_b(w, j, d).wait_send())

        @pl.when(me < n - 1)
        def _():
            halo(w, 0).wait_send()
            halo(w, 1).wait_recv()

        @pl.when(me > 0)
        def _():
            halo(w, 1).wait_send()
            halo(w, 0).wait_recv()


def image_kernel(lags_ref, fields_ref, out_ref):
    lag = lags_ref[pl.program_id(0)]
    for band in range(BANDS):
        total = None
        for w in range(2):
            for c in range(2):
                source = fields_ref[w, 0, c, band, pl.ds(HMAX - lag, ROWS), :]
                receiver = fields_ref[w, 1, c, band, pl.ds(HMAX + lag, ROWS), :]
                term = source * receiver
                total = term if total is None else total + term
        out_ref[0, :, pl.ds(band * LANES, LANES)] = total


def fused(source_field, receiver_field, ref_slowness, omega, interp_index, lags):
    tables = jnp.asarray(fourier_tables())
    vmem = pl.BlockSpec(memory_space=pltpu.VMEM)
    smem = pl.BlockSpec(memory_space=pltpu.SMEM)
    f32 = jnp.float32
    block = (PEERS, 2, ROWS, LANES)
    dma = pltpu.SemaphoreType.DMA
    migrated = pl.pallas_call(
        migrate_kernel,
        out_shape=jax.ShapeDtypeStruct((2, 2, 2, BANDS, ROWS + 2 * HMAX, LANES), f32),
        in_specs=[smem, smem, vmem, vmem, vmem, vmem],
        out_specs=vmem,
        scratch_shapes=[
            pltpu.VMEM((2,) + block, f32),
            pltpu.VMEM((2,) + block, f32),
            pltpu.VMEM((2, 2) + block, f32),
            pltpu.VMEM((2, 2) + block, f32),
            pltpu.VMEM((RADIX, 2, SUB, LANES), f32),
            pltpu.VMEM((2, 2, 2, POINTS, LANES), f32),
            pltpu.VMEM((2, 2, ROWS, POINTS), f32),
            dma((2, PEERS)), dma((2, PEERS)),
            dma((2, 2, PEERS)), dma((2, 2, PEERS)),
            dma((2, 2)), dma((2, 2)),
        ],
        compiler_params=pltpu.CompilerParams(
            collective_id=0, has_side_effects=True, vmem_limit_bytes=56 * 2**20
        ),
    )(omega, ref_slowness, source_field, receiver_field, interp_index, tables)
    count = lags.shape[0]
    return pl.pallas_call(
        image_kernel,
        grid_spec=pltpu.PrefetchScalarGridSpec(
            num_scalar_prefetch=1,
            grid=(count,),
            in_specs=[pl.BlockSpec(migrated.shape, lambda i, lags: (0,) * 6)],
            out_specs=pl.BlockSpec((1, ROWS, POINTS), lambda i, lags: (i, 0, 0)),
        ),
        out_shape=jax.ShapeDtypeStruct((count, ROWS, POINTS), f32),
        compiler_params=pltpu.CompilerParams(vmem_limit_bytes=32 * 2**20),
    )(lags, migrated)


def body(source_field, receiver_field, ref_slowness, omega, interp_index, lags):
    args = (source_field, receiver_field, ref_slowness, omega, interp_index, lags)
    fits = source_field.shape == (2, 2, ROWS, POINTS) and lax.axis_size("lat") == PEERS
    return fused(*args) if fits else local(*args)


def solution(mesh):
    in_specs = (
        P("shots", None, "lat", None),
        P("shots", None, "lat", None),
        P(),
        P(),
        P("lat", None),
        P(),
    )
    out_specs = P("shots", "lat", None)
    return jax.shard_map(body, mesh=mesh, in_specs=in_specs, out_specs=out_specs, check_vma=False)
```

```python
import functools
import math

import jax
import jax.numpy as jnp
import ml_dtypes
import numpy as np
from jax import lax
from jax.experimental import pallas as pl
from jax.experimental.pallas import tpu as pltpu
from jax.sharding import PartitionSpec as P

HMAX = 16
INTERP = 8


depth_step = 2.0
highest = lax.Precision.HIGHEST


def extended(block, sides, width):
    for axis, dim in sides:
        count = lax.axis_size(axis)
        forward = [(i, i + 1) for i in range(count - 1)]
        backward = [(target, source) for source, target in forward]
        low = lax.ppermute(
            lax.slice_in_dim(block, block.shape[dim] - width, None, axis=dim), axis, forward
        )
        high = lax.ppermute(lax.slice_in_dim(block, 0, width, axis=dim), axis, backward)
        block = jnp.concatenate([low, block, high], axis=dim)
    return block


def dft_tables(count):
    index = jnp.arange(count, dtype=jnp.int32)
    turns = index[:, None] * index[None, :] % count
    angle = turns.astype(jnp.float32) * (2.0 * math.pi / count)
    return (jnp.cos(angle), jnp.sin(angle))


def wave_numbers(count):
    index = jnp.arange(count, dtype=jnp.int32)
    signed = jnp.where(index < count // 2, index, index - count)
    return signed.astype(jnp.float32) * (2.0 * math.pi / count)


def factor_pair(count):
    first = 1
    for divisor in range(1, int(math.isqrt(count)) + 1):
        if count % divisor == 0:
            first = divisor
    return (first, count // first)


def complex_apply(real_part, imag_part, cosine, sine, form, sign):
    stacked = jnp.stack([real_part, imag_part], axis=0)
    with_cos = jnp.einsum(form, stacked, cosine, precision=highest)
    with_sin = jnp.einsum(form, stacked, sine, precision=highest)
    return (with_cos[0] - sign * with_sin[1], with_cos[1] + sign * with_sin[0])


def dft_axis(real_part, imag_part, axis, sign, factor):
    count = real_part.shape[axis]
    first, second = factor_pair(count)
    real_part = jnp.moveaxis(real_part, axis, -1)
    imag_part = jnp.moveaxis(imag_part, axis, -1)
    leading = real_part.shape[:-1]
    real_part = real_part.reshape(leading + (first, second))
    imag_part = imag_part.reshape(leading + (first, second))
    cos_a, sin_a = dft_tables(first)
    real_part, imag_part = complex_apply(
        real_part, imag_part, cos_a, sin_a, "...ab,ac->...cb", sign
    )
    row_index = jnp.arange(first, dtype=jnp.int32)[:, None]
    col_index = jnp.arange(second, dtype=jnp.int32)[None, :]
    twist = (row_index * col_index % count).astype(jnp.float32) * (2.0 * math.pi / count)
    cos_t = jnp.cos(twist)
    sin_t = sign * jnp.sin(twist)
    real_part, imag_part = (
        real_part * cos_t - imag_part * sin_t,
        real_part * sin_t + imag_part * cos_t,
    )
    cos_b, sin_b = dft_tables(second)
    real_part, imag_part = complex_apply(
        real_part, imag_part, cos_b, sin_b, "...cb,bd->...cd", sign
    )
    real_part = jnp.swapaxes(real_part, -1, -2).reshape(leading + (count,)) * factor
    imag_part = jnp.swapaxes(imag_part, -1, -2).reshape(leading + (count,)) * factor
    return (jnp.moveaxis(real_part, -1, axis), jnp.moveaxis(imag_part, -1, axis))


def send_out_each(spectrum):
    return lax.all_to_all(spectrum, "lat", split_axis=4, concat_axis=3, tiled=True)


def send_back_each(fields):
    return lax.all_to_all(fields, "lat", split_axis=4, concat_axis=5, tiled=True)


def propagate(fields, omegas, ref_slowness, send_out, send_back):
    n_y = fields.shape[4]
    n_x = fields.shape[3] * lax.axis_size("lat")
    real_part, imag_part = dft_axis(fields[:, :, 0], fields[:, :, 1], 3, -1.0, 1.0)
    turned = send_out(jnp.stack([real_part, imag_part], axis=2))
    n_cols = turned.shape[4]
    real_part, imag_part = dft_axis(turned[:, :, 0], turned[:, :, 1], 2, -1.0, 1.0)
    real_part = jnp.swapaxes(real_part, 2, 3)
    imag_part = jnp.swapaxes(imag_part, 2, 3)
    ky_all = wave_numbers(n_y)
    ky = lax.dynamic_slice_in_dim(ky_all, lax.axis_index("lat") * n_cols, n_cols)
    kx = wave_numbers(n_x)
    lateral = ky[:, None] ** 2 + kx[None, :] ** 2
    direction = jnp.array([-1.0, 1.0], dtype=jnp.float32)[:, None, None, None]
    shifted = []
    for j in range(2):
        vertical = (omegas * ref_slowness[j]) ** 2
        arg = vertical[:, None, None] - lateral[None]
        phase = jnp.sqrt(jnp.maximum(arg, 0.0)) * depth_step
        decay = jnp.exp(-jnp.sqrt(jnp.maximum(-arg, 0.0)) * depth_step)
        cos_shift = (decay * jnp.cos(phase))[None]
        sin_shift = direction * (decay * jnp.sin(phase))[None]
        new_real = real_part * cos_shift - imag_part * sin_shift
        new_imag = real_part * sin_shift + imag_part * cos_shift
        back_real, back_imag = dft_axis(new_real, new_imag, 3, 1.0, 1.0 / n_x)
        back_real = jnp.swapaxes(back_real, 2, 3)
        back_imag = jnp.swapaxes(back_imag, 2, 3)
        shifted.append(jnp.stack([back_real, back_imag], axis=2))
    returned = send_back(jnp.stack(shifted, axis=0))
    out_real, out_imag = dft_axis(returned[:, :, :, 0], returned[:, :, :, 1], 4, 1.0, 1.0 / n_y)
    return jnp.stack([out_real, out_imag], axis=3)


def local(source_field, receiver_field, ref_slowness, omega, interp_index, lags):
    fields = jnp.stack([source_field, receiver_field], axis=0)
    pieces = []
    for step in range(fields.shape[1]):
        pieces.append(
            propagate(
                fields[:, step : step + 1],
                omega[step : step + 1],
                ref_slowness,
                send_out_each,
                send_back_each,
            )
        )
    references = jnp.concatenate(pieces, axis=2)
    weight = interp_index.astype(jnp.float32) / (INTERP - 1)
    migrated = (1.0 - weight) * references[0] + weight * references[1]
    padded = extended(migrated, (("lat", 3),), HMAX)
    rows = migrated.shape[3]

    def one_offset(lag):
        source_rows = lax.dynamic_slice_in_dim(padded[0], HMAX - lag, rows, 2)
        receiver_rows = lax.dynamic_slice_in_dim(padded[1], HMAX + lag, rows, 2)
        return jnp.sum(source_rows * receiver_rows, axis=(0, 1))

    return lax.map(one_offset, lags)


RADIX = 4
SUB = 256
POINTS = RADIX * SUB
PEERS = 16
ROWS = POINTS // PEERS
LANES = 2 * ROWS
BANDS = POINTS // LANES
HALF = PEERS // 2
GROUPS = 4
INNER = 3
OUTER = GROUPS - INNER
SLOTS = max(INNER, OUTER)
MESH = pl.DeviceIdType.MESH


def fourier_tables():
    r = np.arange(RADIX)[:, None, None]
    m = np.arange(SUB)[None, :, None]
    y = np.arange(SUB)[None, None, :]
    angle = ((r + RADIX * m) * y % POINTS) * (2.0 * np.pi / POINTS)
    both = np.stack([np.cos(angle), np.sin(angle)], axis=1).astype(np.float32)
    high = both.astype(ml_dtypes.bfloat16)
    low = (both - high.astype(np.float32)).astype(ml_dtypes.bfloat16)
    straight = np.stack([high, low], axis=2)
    return np.stack([straight, np.swapaxes(straight, -1, -2)])


def split(value):
    high = value.astype(jnp.bfloat16)
    low = (value - high.astype(jnp.float32)).astype(jnp.bfloat16)
    return high, low


def dot(a, b):
    return jnp.dot(a, b, preferred_element_type=jnp.float32)


def table_left(tab_ref, turned, r, trig, pair):
    high, low = tab_ref[turned, r, trig, 0], tab_ref[turned, r, trig, 1]
    return dot(high, pair[0]) + (dot(high, pair[1]) + dot(low, pair[0]))


def table_right(tab_ref, turned, r, trig, pair):
    high, low = tab_ref[turned, r, trig, 0], tab_ref[turned, r, trig, 1]
    return dot(pair[0], high) + (dot(pair[1], high) + dot(pair[0], low))


def forward_four(re, im):
    pr, mr, qr, nr = re[0] + re[2], re[0] - re[2], re[1] + re[3], re[1] - re[3]
    pi, mi, qi, ni = im[0] + im[2], im[0] - im[2], im[1] + im[3], im[1] - im[3]
    return (
        [pr + qr, mr + ni, pr - qr, mr - ni],
        [pi + qi, mi - nr, pi - qi, mi + nr],
    )


def backward_four(re, im):
    pr, mr, qr, nr = re[0] + re[2], re[0] - re[2], re[1] + re[3], re[1] - re[3]
    pi, mi, qi, ni = im[0] + im[2], im[0] - im[2], im[1] + im[3], im[1] - im[3]
    return (
        [pr + qr, mr - ni, pr - qr, mr + ni],
        [pi + qi, mi + nr, pi - qi, mi - nr],
    )


def signed_wave(index):
    signed = jnp.where(index < POINTS // 2, index, index - POINTS)
    return signed.astype(jnp.float32) * (2.0 * math.pi / POINTS)


def series(square, terms):
    total = jnp.full_like(square, terms[-1])
    for term in terms[-2::-1]:
        total = total * square + term
    return total


SIN_TERMS = [(-1.0) ** i / math.factorial(2 * i + 1) for i in range(8)]
COS_TERMS = [(-1.0) ** i / math.factorial(2 * i) for i in range(8)]


def shift_pair(arg):
    root = jnp.sqrt(jnp.abs(arg))
    half = root - 0.5 * math.pi
    square = half * half
    sine = half * series(square, SIN_TERMS)
    cosine = series(square, COS_TERMS)
    moving = arg > 0.0
    decay = jnp.exp(-depth_step * root)
    real = jnp.where(moving, 2.0 * sine * sine - 1.0, decay)
    imag = jnp.where(moving, -2.0 * sine * cosine, 0.0)
    return real, imag


def halves(first, second, low_half):
    low = jnp.where(low_half, first, pltpu.roll(second, ROWS, 1))
    high = jnp.where(low_half, pltpu.roll(first, ROWS, 1), second)
    return low, high


def migrate_kernel(
    omega_ref, slow_ref, src_ref, rec_ref, index_ref, tab_ref, out_ref,
    send_f, recv_f, send_b, recv_b, spec, shift, first_ref,
    sem_fs, sem_fr, sem_bs, sem_br, sem_hs, sem_hr,
):
    me = lax.axis_index("lat")
    n = PEERS
    lane = lax.broadcasted_iota(jnp.int32, (ROWS, LANES), 1)
    low_half = lane < ROWS

    half = me // HALF
    pos = lax.rem(me, HALF)
    plane = me // GROUPS
    along = lax.rem(me, GROUPS)
    inside = (plane == 1) | (plane == 2)
    slots = jnp.where(inside, INNER, OUTER)
    base = jnp.where(inside, 0, INNER)

    def owner(group, i, hf):
        return GROUPS * jnp.where(group < INNER, 1 + hf, 3 * hf) + i

    def copy_f(w, group, i, hf):
        slot = group if group < INNER else group - INNER
        block = GROUPS * group + i
        return pltpu.make_async_remote_copy(
            src_ref=send_f.at[w, block], dst_ref=recv_f.at[w, slot, me],
            send_sem=sem_fs.at[w, block, hf], recv_sem=sem_fr.at[w, slot, me],
            device_id={"lat": owner(group, i, hf)}, device_id_type=MESH,
        )

    def each_f(w, group, body):
        @pl.loop(0, HALF)
        def _(e):
            i = lax.rem(e + along, GROUPS)
            hf = lax.rem(e // GROUPS + 1 + half, 2)

            @pl.when(owner(group, i, hf) != me)
            def _():
                body(copy_f(w, group, i, hf))

    def start_f(w, group):
        each_f(w, group, lambda copy: copy.start())

        @pl.when(owner(group, along, half) == me)
        def _():
            slot = group if group < INNER else group - INNER
            recv_f[w, slot, me] = send_f[w, GROUPS * group + along]

    def wait_f(w, slot):
        @pl.loop(1, PEERS)
        def _(d):
            origin = lax.rem(me + PEERS - d, PEERS)
            pltpu.make_async_remote_copy(
                src_ref=send_f.at[w, 0], dst_ref=recv_f.at[w, slot, origin],
                send_sem=sem_fs.at[w, 0, 0], recv_sem=sem_fr.at[w, slot, origin],
                device_id={"lat": origin}, device_id_type=MESH,
            ).wait_recv()

    def each_b(w, slot, j, body):
        block = GROUPS * (base + slot) + along

        @pl.loop(1, HALF)
        def _(e):
            t = lax.rem(pos + e, HALF)
            body(pltpu.make_async_remote_copy(
                src_ref=send_b.at[w, slot, j, t], dst_ref=recv_b.at[w, j, block],
                send_sem=sem_bs.at[w, slot, j, t], recv_sem=sem_br.at[w, j, block],
                device_id={"lat": HALF * half + t}, device_id_type=MESH,
            ))

    def start_b(w, slot, j):
        each_b(w, slot, j, lambda copy: copy.start())
        recv_b[w, j, GROUPS * (base + slot) + along] = send_b[w, slot, j, pos]

    def wait_b(w, j):
        @pl.loop(0, PEERS)
        def _(block):
            origin = owner(block // GROUPS, lax.rem(block, GROUPS), half)

            @pl.when(origin != me)
            def _():
                pltpu.make_async_remote_copy(
                    src_ref=send_b.at[w, 0, j, 0], dst_ref=recv_b.at[w, j, block],
                    send_sem=sem_bs.at[w, 0, j, 0], recv_sem=sem_br.at[w, j, block],
                    device_id={"lat": origin}, device_id_type=MESH,
                ).wait_recv()

    def halo(w, side):
        to, take, put = (me + 1, ROWS, 0) if side == 0 else (me - 1, HMAX, HMAX + ROWS)
        return pltpu.make_async_remote_copy(
            src_ref=out_ref.at[w, :, :, :, pl.ds(take, HMAX), :],
            dst_ref=out_ref.at[w, :, :, :, pl.ds(put, HMAX), :],
            send_sem=sem_hs.at[w, side], recv_sem=sem_hr.at[w, side],
            device_id={"lat": to}, device_id_type=MESH,
        )

    def every(body):
        @pl.loop(1, n)
        def _(d):
            body(d)

    barrier = pltpu.get_barrier_semaphore()

    def greet(d):
        pl.semaphore_signal(
            barrier, inc=1, device_id={"lat": lax.rem(me + d, n)}, device_id_type=MESH
        )

    every(greet)

    def rows_forward(w, ready):
        re, im = [], []
        for q in range(RADIX):
            cut = pl.ds(q * SUB, SUB)
            re.append(jnp.concatenate([src_ref[w, 0, :, cut], rec_ref[w, 0, :, cut]], axis=0))
            im.append(jnp.concatenate([src_ref[w, 1, :, cut], rec_ref[w, 1, :, cut]], axis=0))
        re, im = forward_four(re, im)
        for r in range(RADIX):
            pair = split(jnp.concatenate([re[r], im[r]], axis=0))
            with_cos = table_right(tab_ref, 1, r, 0, pair)
            with_sin = table_right(tab_ref, 1, r, 1, pair)
            parts = (
                with_cos[:LANES] + with_sin[LANES:],
                with_cos[LANES:] - with_sin[:LANES],
            )
            for c in range(2):
                for b in range(2):
                    piece = parts[c][:, b * LANES : (b + 1) * LANES]
                    low, high = halves(piece[:ROWS], piece[ROWS:], low_half)
                    peer = RADIX * r + 2 * b
                    send_f[w, peer, c] = low
                    send_f[w, peer + 1, c] = high
            if w == 0 and r == 0:
                ready()
            start_f(w, r)

    def make_shift(w, slot, j):
        speed = omega_ref[w] * slow_ref[j]
        vertical = speed * speed
        wide = lax.broadcasted_iota(jnp.int32, (ROWS, LANES), 1)
        tall = lax.broadcasted_iota(jnp.int32, (ROWS, LANES), 0)
        place = ROWS * (GROUPS * (base + slot) + along) + lax.rem(wide, ROWS)
        ky = signed_wave(place // SUB + RADIX * lax.rem(place, SUB))
        ky2 = ky * ky
        sign = jnp.where(wide < ROWS, -1.0, 1.0)
        scale = 1.0 / (POINTS * POINTS)

        @pl.loop(0, PEERS)
        def _(block):
            at = ROWS * block
            r = at // SUB
            kx = signed_wave(r + RADIX * (lax.rem(at, SUB) + tall))
            real, imag = shift_pair(vertical - (kx * kx + ky2))
            rows = pl.ds(pl.multiple_of(ROWS * block, ROWS), ROWS)
            shift[j, 0, rows, :] = real * scale
            shift[j, 1, rows, :] = imag * (sign * scale)

    def columns_forward(w, slot):
        re, im = [], []
        for q in range(RADIX):
            re.append(recv_f[w, slot, 4 * q : 4 * q + 4, 0].reshape(SUB, LANES))
            im.append(recv_f[w, slot, 4 * q : 4 * q + 4, 1].reshape(SUB, LANES))
        re, im = forward_four(re, im)
        for r in range(RADIX):
            pair = split(jnp.concatenate([re[r], im[r]], axis=1))
            with_cos = table_left(tab_ref, 0, r, 0, pair)
            with_sin = table_left(tab_ref, 0, r, 1, pair)
            spec[r, 0] = with_cos[:, :LANES] + with_sin[:, LANES:]
            spec[r, 1] = with_cos[:, LANES:] - with_sin[:, :LANES]

    def columns_backward(w, slot, j):
        re, im = [], []
        for r in range(RADIX):
            cos_shift = shift[j, 0, pl.ds(r * SUB, SUB), :]
            sin_shift = shift[j, 1, pl.ds(r * SUB, SUB), :]
            new_re = spec[r, 0] * cos_shift - spec[r, 1] * sin_shift
            new_im = spec[r, 0] * sin_shift + spec[r, 1] * cos_shift
            pair = split(jnp.concatenate([new_re, new_im], axis=1))
            with_cos = table_left(tab_ref, 1, r, 0, pair)
            with_sin = table_left(tab_ref, 1, r, 1, pair)
            re.append(with_cos[:, :LANES] - with_sin[:, LANES:])
            im.append(with_cos[:, LANES:] + with_sin[:, :LANES])
        flip = (1 - 2 * half).astype(jnp.float32)
        first = [a + b + flip * (c + d) for a, b, c, d in (
            (re[0], re[2], re[1], re[3]), (im[0], im[2], im[1], im[3]))]
        second = [
            re[0] - re[2] - flip * (im[1] - im[3]),
            im[0] - im[2] + flip * (re[1] - re[3]),
        ]
        for c in range(2):
            send_b[w, slot, j, 0:4, c] = first[c].reshape(4, ROWS, LANES)
            send_b[w, slot, j, 4:8, c] = second[c].reshape(4, ROWS, LANES)

    def rows_backward(w, j):
        re, im = [], []
        for r in range(RADIX):
            stacked = []
            for c in range(2):
                sides = [
                    halves(recv_b[w, j, 4 * r + 2 * b, c], recv_b[w, j, 4 * r + 2 * b + 1, c], low_half)
                    for b in range(2)
                ]
                for field in range(2):
                    stacked.append(jnp.concatenate([sides[0][field], sides[1][field]], axis=1))
            pair = split(jnp.concatenate(stacked, axis=0))
            with_cos = table_right(tab_ref, 0, r, 0, pair)
            with_sin = table_right(tab_ref, 0, r, 1, pair)
            re.append(with_cos[:LANES] - with_sin[LANES:])
            im.append(with_cos[LANES:] + with_sin[:LANES])
        parts = backward_four(re, im)
        for q in range(RADIX):
            cut = pl.ds(q * SUB, SUB)
            weight = index_ref[:, cut].astype(jnp.float32) / (INTERP - 1)
            for c in range(2):
                for field in range(2):
                    value = parts[c][q][ROWS * field : ROWS * (field + 1)]
                    if j == 0:
                        first_ref[field, c, :, cut] = (1.0 - weight) * value
                    else:
                        mixed = first_ref[field, c, :, cut] + weight * value
                        for b in range(2):
                            out_ref[w, field, c, 2 * q + b, pl.ds(HMAX, ROWS), :] = (
                                mixed[:, b * LANES : (b + 1) * LANES]
                            )

    @pl.when(me == 0)
    def _():
        for w in range(2):
            out_ref[w, :, :, :, pl.ds(0, HMAX), :] = jnp.zeros((2, 2, BANDS, HMAX, LANES), jnp.float32)

    @pl.when(me == n - 1)
    def _():
        for w in range(2):
            out_ref[w, :, :, :, pl.ds(HMAX + ROWS, HMAX), :] = jnp.zeros((2, 2, BANDS, HMAX, LANES), jnp.float32)

    rows_forward(0, lambda: pl.semaphore_wait(barrier, n - 1))
    rows_forward(1, None)

    @pl.loop(0, 2 * slots)
    def _(chunk):
        w = jnp.where(chunk < slots, 0, 1)
        slot = chunk - slots * w
        for j in range(2):
            make_shift(w, slot, j)
        wait_f(w, slot)
        columns_forward(w, slot)
        for j in range(2):
            columns_backward(w, slot, j)
            start_b(w, slot, j)

    for w in range(2):
        for j in range(2):
            wait_b(w, j)
            rows_backward(w, j)

        @pl.when(me < n - 1)
        def _():
            halo(w, 0).start()

        @pl.when(me > 0)
        def _():
            halo(w, 1).start()

    for w in range(2):
        for group in range(GROUPS):
            each_f(w, group, lambda copy: copy.wait_send())

        @pl.loop(0, slots)
        def _(slot):
            for j in range(2):
                each_b(w, slot, j, lambda copy: copy.wait_send())

        @pl.when(me < n - 1)
        def _():
            halo(w, 0).wait_send()
            halo(w, 1).wait_recv()

        @pl.when(me > 0)
        def _():
            halo(w, 1).wait_send()
            halo(w, 0).wait_recv()


def image_kernel(lags_ref, fields_ref, out_ref):
    lag = lags_ref[pl.program_id(0)]
    for band in range(BANDS):
        total = None
        for w in range(2):
            for c in range(2):
                source = fields_ref[w, 0, c, band, pl.ds(HMAX - lag, ROWS), :]
                receiver = fields_ref[w, 1, c, band, pl.ds(HMAX + lag, ROWS), :]
                term = source * receiver
                total = term if total is None else total + term
        out_ref[0, :, pl.ds(band * LANES, LANES)] = total


def fused(source_field, receiver_field, ref_slowness, omega, interp_index, lags):
    tables = jnp.asarray(fourier_tables())
    vmem = pl.BlockSpec(memory_space=pltpu.VMEM)
    smem = pl.BlockSpec(memory_space=pltpu.SMEM)
    f32 = jnp.float32
    block = (PEERS, 2, ROWS, LANES)
    dma = pltpu.SemaphoreType.DMA
    migrated = pl.pallas_call(
        migrate_kernel,
        out_shape=jax.ShapeDtypeStruct((2, 2, 2, BANDS, ROWS + 2 * HMAX, LANES), f32),
        in_specs=[smem, smem, vmem, vmem, vmem, vmem],
        out_specs=vmem,
        scratch_shapes=[
            pltpu.VMEM((2,) + block, f32),
            pltpu.VMEM((2, SLOTS) + block, f32),
            pltpu.VMEM((2, SLOTS, 2, HALF) + block[1:], f32),
            pltpu.VMEM((2, 2) + block, f32),
            pltpu.VMEM((RADIX, 2, SUB, LANES), f32),
            pltpu.VMEM((2, 2, POINTS, LANES), f32),
            pltpu.VMEM((2, 2, ROWS, POINTS), f32),
            dma((2, PEERS, 2)), dma((2, SLOTS, PEERS)),
            dma((2, SLOTS, 2, HALF)), dma((2, 2, PEERS)),
            dma((2, 2)), dma((2, 2)),
        ],
        compiler_params=pltpu.CompilerParams(
            collective_id=0, has_side_effects=True, vmem_limit_bytes=56 * 2**20
        ),
    )(omega, ref_slowness, source_field, receiver_field, interp_index, tables)
    count = lags.shape[0]
    return pl.pallas_call(
        image_kernel,
        grid_spec=pltpu.PrefetchScalarGridSpec(
            num_scalar_prefetch=1,
            grid=(count,),
            in_specs=[pl.BlockSpec(migrated.shape, lambda i, lags: (0,) * 6)],
            out_specs=pl.BlockSpec((1, ROWS, POINTS), lambda i, lags: (i, 0, 0)),
        ),
        out_shape=jax.ShapeDtypeStruct((count, ROWS, POINTS), f32),
        compiler_params=pltpu.CompilerParams(vmem_limit_bytes=32 * 2**20),
    )(lags, migrated)


def body(source_field, receiver_field, ref_slowness, omega, interp_index, lags):
    args = (source_field, receiver_field, ref_slowness, omega, interp_index, lags)
    fits = source_field.shape == (2, 2, ROWS, POINTS) and lax.axis_size("lat") == PEERS
    return fused(*args) if fits else local(*args)


def solution(mesh):
    in_specs = (
        P("shots", None, "lat", None),
        P("shots", None, "lat", None),
        P(),
        P(),
        P("lat", None),
        P(),
    )
    out_specs = P("shots", "lat", None)
    return jax.shard_map(body, mesh=mesh, in_specs=in_specs, out_specs=out_specs, check_vma=False)
```

```python
import functools
import math

import jax
import jax.numpy as jnp
import ml_dtypes
import numpy as np
from jax import lax
from jax.experimental import pallas as pl
from jax.experimental.pallas import tpu as pltpu
from jax.sharding import PartitionSpec as P

HMAX = 16
INTERP = 8


depth_step = 2.0
highest = lax.Precision.HIGHEST


def extended(block, sides, width):
    for axis, dim in sides:
        count = lax.axis_size(axis)
        forward = [(i, i + 1) for i in range(count - 1)]
        backward = [(target, source) for source, target in forward]
        low = lax.ppermute(
            lax.slice_in_dim(block, block.shape[dim] - width, None, axis=dim), axis, forward
        )
        high = lax.ppermute(lax.slice_in_dim(block, 0, width, axis=dim), axis, backward)
        block = jnp.concatenate([low, block, high], axis=dim)
    return block


def dft_tables(count):
    index = jnp.arange(count, dtype=jnp.int32)
    turns = index[:, None] * index[None, :] % count
    angle = turns.astype(jnp.float32) * (2.0 * math.pi / count)
    return (jnp.cos(angle), jnp.sin(angle))


def wave_numbers(count):
    index = jnp.arange(count, dtype=jnp.int32)
    signed = jnp.where(index < count // 2, index, index - count)
    return signed.astype(jnp.float32) * (2.0 * math.pi / count)


def factor_pair(count):
    first = 1
    for divisor in range(1, int(math.isqrt(count)) + 1):
        if count % divisor == 0:
            first = divisor
    return (first, count // first)


def complex_apply(real_part, imag_part, cosine, sine, form, sign):
    stacked = jnp.stack([real_part, imag_part], axis=0)
    with_cos = jnp.einsum(form, stacked, cosine, precision=highest)
    with_sin = jnp.einsum(form, stacked, sine, precision=highest)
    return (with_cos[0] - sign * with_sin[1], with_cos[1] + sign * with_sin[0])


def dft_axis(real_part, imag_part, axis, sign, factor):
    count = real_part.shape[axis]
    first, second = factor_pair(count)
    real_part = jnp.moveaxis(real_part, axis, -1)
    imag_part = jnp.moveaxis(imag_part, axis, -1)
    leading = real_part.shape[:-1]
    real_part = real_part.reshape(leading + (first, second))
    imag_part = imag_part.reshape(leading + (first, second))
    cos_a, sin_a = dft_tables(first)
    real_part, imag_part = complex_apply(
        real_part, imag_part, cos_a, sin_a, "...ab,ac->...cb", sign
    )
    row_index = jnp.arange(first, dtype=jnp.int32)[:, None]
    col_index = jnp.arange(second, dtype=jnp.int32)[None, :]
    twist = (row_index * col_index % count).astype(jnp.float32) * (2.0 * math.pi / count)
    cos_t = jnp.cos(twist)
    sin_t = sign * jnp.sin(twist)
    real_part, imag_part = (
        real_part * cos_t - imag_part * sin_t,
        real_part * sin_t + imag_part * cos_t,
    )
    cos_b, sin_b = dft_tables(second)
    real_part, imag_part = complex_apply(
        real_part, imag_part, cos_b, sin_b, "...cb,bd->...cd", sign
    )
    real_part = jnp.swapaxes(real_part, -1, -2).reshape(leading + (count,)) * factor
    imag_part = jnp.swapaxes(imag_part, -1, -2).reshape(leading + (count,)) * factor
    return (jnp.moveaxis(real_part, -1, axis), jnp.moveaxis(imag_part, -1, axis))


def send_out_each(spectrum):
    return lax.all_to_all(spectrum, "lat", split_axis=4, concat_axis=3, tiled=True)


def send_back_each(fields):
    return lax.all_to_all(fields, "lat", split_axis=4, concat_axis=5, tiled=True)


def propagate(fields, omegas, ref_slowness, send_out, send_back):
    n_y = fields.shape[4]
    n_x = fields.shape[3] * lax.axis_size("lat")
    real_part, imag_part = dft_axis(fields[:, :, 0], fields[:, :, 1], 3, -1.0, 1.0)
    turned = send_out(jnp.stack([real_part, imag_part], axis=2))
    n_cols = turned.shape[4]
    real_part, imag_part = dft_axis(turned[:, :, 0], turned[:, :, 1], 2, -1.0, 1.0)
    real_part = jnp.swapaxes(real_part, 2, 3)
    imag_part = jnp.swapaxes(imag_part, 2, 3)
    ky_all = wave_numbers(n_y)
    ky = lax.dynamic_slice_in_dim(ky_all, lax.axis_index("lat") * n_cols, n_cols)
    kx = wave_numbers(n_x)
    lateral = ky[:, None] ** 2 + kx[None, :] ** 2
    direction = jnp.array([-1.0, 1.0], dtype=jnp.float32)[:, None, None, None]
    shifted = []
    for j in range(2):
        vertical = (omegas * ref_slowness[j]) ** 2
        arg = vertical[:, None, None] - lateral[None]
        phase = jnp.sqrt(jnp.maximum(arg, 0.0)) * depth_step
        decay = jnp.exp(-jnp.sqrt(jnp.maximum(-arg, 0.0)) * depth_step)
        cos_shift = (decay * jnp.cos(phase))[None]
        sin_shift = direction * (decay * jnp.sin(phase))[None]
        new_real = real_part * cos_shift - imag_part * sin_shift
        new_imag = real_part * sin_shift + imag_part * cos_shift
        back_real, back_imag = dft_axis(new_real, new_imag, 3, 1.0, 1.0 / n_x)
        back_real = jnp.swapaxes(back_real, 2, 3)
        back_imag = jnp.swapaxes(back_imag, 2, 3)
        shifted.append(jnp.stack([back_real, back_imag], axis=2))
    returned = send_back(jnp.stack(shifted, axis=0))
    out_real, out_imag = dft_axis(returned[:, :, :, 0], returned[:, :, :, 1], 4, 1.0, 1.0 / n_y)
    return jnp.stack([out_real, out_imag], axis=3)


def local(source_field, receiver_field, ref_slowness, omega, interp_index, lags):
    fields = jnp.stack([source_field, receiver_field], axis=0)
    pieces = []
    for step in range(fields.shape[1]):
        pieces.append(
            propagate(
                fields[:, step : step + 1],
                omega[step : step + 1],
                ref_slowness,
                send_out_each,
                send_back_each,
            )
        )
    references = jnp.concatenate(pieces, axis=2)
    weight = interp_index.astype(jnp.float32) / (INTERP - 1)
    migrated = (1.0 - weight) * references[0] + weight * references[1]
    padded = extended(migrated, (("lat", 3),), HMAX)
    rows = migrated.shape[3]

    def one_offset(lag):
        source_rows = lax.dynamic_slice_in_dim(padded[0], HMAX - lag, rows, 2)
        receiver_rows = lax.dynamic_slice_in_dim(padded[1], HMAX + lag, rows, 2)
        return jnp.sum(source_rows * receiver_rows, axis=(0, 1))

    return lax.map(one_offset, lags)


RADIX = 4
SUB = 256
POINTS = RADIX * SUB
PEERS = 16
ROWS = POINTS // PEERS
LANES = 2 * ROWS
BANDS = POINTS // LANES
HALF = PEERS // 2
GROUPS = 4
INNER = 3
OUTER = GROUPS - INNER
SLOTS = max(INNER, OUTER)
MESH = pl.DeviceIdType.MESH


def fourier_tables():
    r = np.arange(RADIX)[:, None, None]
    m = np.arange(SUB)[None, :, None]
    y = np.arange(SUB)[None, None, :]
    angle = ((r + RADIX * m) * y % POINTS) * (2.0 * np.pi / POINTS)
    both = np.stack([np.cos(angle), np.sin(angle)], axis=1).astype(np.float32)
    high = both.astype(ml_dtypes.bfloat16)
    low = (both - high.astype(np.float32)).astype(ml_dtypes.bfloat16)
    straight = np.stack([high, low], axis=2)
    return np.stack([straight, np.swapaxes(straight, -1, -2)])


def split(value):
    high = value.astype(jnp.bfloat16)
    low = (value - high.astype(jnp.float32)).astype(jnp.bfloat16)
    return high, low


def dot(a, b):
    return jnp.dot(a, b, preferred_element_type=jnp.float32)


def table_left(tab_ref, turned, r, trig, pair):
    high, low = tab_ref[turned, r, trig, 0], tab_ref[turned, r, trig, 1]
    return dot(high, pair[0]) + (dot(high, pair[1]) + dot(low, pair[0]))


def table_right(tab_ref, turned, r, trig, pair):
    high, low = tab_ref[turned, r, trig, 0], tab_ref[turned, r, trig, 1]
    return dot(pair[0], high) + (dot(pair[1], high) + dot(pair[0], low))


def forward_four(re, im):
    pr, mr, qr, nr = re[0] + re[2], re[0] - re[2], re[1] + re[3], re[1] - re[3]
    pi, mi, qi, ni = im[0] + im[2], im[0] - im[2], im[1] + im[3], im[1] - im[3]
    return (
        [pr + qr, mr + ni, pr - qr, mr - ni],
        [pi + qi, mi - nr, pi - qi, mi + nr],
    )


def backward_four(re, im):
    pr, mr, qr, nr = re[0] + re[2], re[0] - re[2], re[1] + re[3], re[1] - re[3]
    pi, mi, qi, ni = im[0] + im[2], im[0] - im[2], im[1] + im[3], im[1] - im[3]
    return (
        [pr + qr, mr - ni, pr - qr, mr + ni],
        [pi + qi, mi + nr, pi - qi, mi - nr],
    )


def signed_wave(index):
    signed = jnp.where(index < POINTS // 2, index, index - POINTS)
    return signed.astype(jnp.float32) * (2.0 * math.pi / POINTS)


def series(square, terms):
    total = jnp.full_like(square, terms[-1])
    for term in terms[-2::-1]:
        total = total * square + term
    return total


SIN_TERMS = [(-1.0) ** i / math.factorial(2 * i + 1) for i in range(8)]
COS_TERMS = [(-1.0) ** i / math.factorial(2 * i) for i in range(8)]


def shift_pair(arg):
    root = jnp.sqrt(jnp.abs(arg))
    half = root - 0.5 * math.pi
    square = half * half
    sine = half * series(square, SIN_TERMS)
    cosine = series(square, COS_TERMS)
    moving = arg > 0.0
    decay = jnp.exp(-depth_step * root)
    real = jnp.where(moving, 2.0 * sine * sine - 1.0, decay)
    imag = jnp.where(moving, -2.0 * sine * cosine, 0.0)
    return real, imag


def halves(first, second, low_half):
    low = jnp.where(low_half, first, pltpu.roll(second, ROWS, 1))
    high = jnp.where(low_half, pltpu.roll(first, ROWS, 1), second)
    return low, high


def migrate_kernel(
    omega_ref, slow_ref, src_ref, rec_ref, index_ref, tab_ref, out_ref,
    send_f, recv_f, send_b, recv_b, spec, shift, first_ref,
    sem_fs, sem_fr, sem_bs, sem_br, sem_hs, sem_hr,
):
    me = lax.axis_index("lat")
    n = PEERS
    lane = lax.broadcasted_iota(jnp.int32, (ROWS, LANES), 1)
    low_half = lane < ROWS

    half = me // HALF
    pos = lax.rem(me, HALF)
    plane = me // GROUPS
    along = lax.rem(me, GROUPS)
    inside = (plane == 1) | (plane == 2)
    slots = jnp.where(inside, INNER, OUTER)
    base = jnp.where(inside, 0, INNER)

    def owner(group, i, hf):
        return GROUPS * jnp.where(group < INNER, 1 + hf, 3 * hf) + i

    def copy_f(w, group, i, hf):
        slot = group if group < INNER else group - INNER
        block = GROUPS * group + i
        return pltpu.make_async_remote_copy(
            src_ref=send_f.at[w, block], dst_ref=recv_f.at[w, slot, me],
            send_sem=sem_fs.at[w, block, hf], recv_sem=sem_fr.at[w, slot, me],
            device_id={"lat": owner(group, i, hf)}, device_id_type=MESH,
        )

    def each_f(w, group, body):
        @pl.loop(0, HALF)
        def _(e):
            i = lax.rem(e + along, GROUPS)
            hf = lax.rem(e // GROUPS + 1 + half, 2)

            @pl.when(owner(group, i, hf) != me)
            def _():
                body(copy_f(w, group, i, hf))

    def start_f(w, group):
        each_f(w, group, lambda copy: copy.start())

        @pl.when(owner(group, along, half) == me)
        def _():
            slot = group if group < INNER else group - INNER
            recv_f[w, slot, me] = send_f[w, GROUPS * group + along]

    def wait_f(w, slot):
        @pl.loop(1, PEERS)
        def _(d):
            origin = lax.rem(me + PEERS - d, PEERS)
            pltpu.make_async_remote_copy(
                src_ref=send_f.at[w, 0], dst_ref=recv_f.at[w, slot, origin],
                send_sem=sem_fs.at[w, 0, 0], recv_sem=sem_fr.at[w, slot, origin],
                device_id={"lat": origin}, device_id_type=MESH,
            ).wait_recv()

    def each_b(w, slot, j, body):
        block = GROUPS * (base + slot) + along

        @pl.loop(1, HALF)
        def _(e):
            t = lax.rem(pos + e, HALF)
            body(pltpu.make_async_remote_copy(
                src_ref=send_b.at[w, slot, j, t], dst_ref=recv_b.at[w, j, block],
                send_sem=sem_bs.at[w, slot, j, t], recv_sem=sem_br.at[w, j, block],
                device_id={"lat": HALF * half + t}, device_id_type=MESH,
            ))

    def start_b(w, slot, j):
        each_b(w, slot, j, lambda copy: copy.start())
        recv_b[w, j, GROUPS * (base + slot) + along] = send_b[w, slot, j, pos]

    def wait_b(w, j):
        @pl.loop(0, PEERS)
        def _(block):
            origin = owner(block // GROUPS, lax.rem(block, GROUPS), half)

            @pl.when(origin != me)
            def _():
                pltpu.make_async_remote_copy(
                    src_ref=send_b.at[w, 0, j, 0], dst_ref=recv_b.at[w, j, block],
                    send_sem=sem_bs.at[w, 0, j, 0], recv_sem=sem_br.at[w, j, block],
                    device_id={"lat": origin}, device_id_type=MESH,
                ).wait_recv()

    def halo(w, side):
        to, take, put = (me + 1, ROWS, 0) if side == 0 else (me - 1, HMAX, HMAX + ROWS)
        return pltpu.make_async_remote_copy(
            src_ref=out_ref.at[w, :, :, :, pl.ds(take, HMAX), :],
            dst_ref=out_ref.at[w, :, :, :, pl.ds(put, HMAX), :],
            send_sem=sem_hs.at[w, side], recv_sem=sem_hr.at[w, side],
            device_id={"lat": to}, device_id_type=MESH,
        )

    def every(body):
        @pl.loop(1, n)
        def _(d):
            body(d)

    barrier = pltpu.get_barrier_semaphore()

    def greet(d):
        pl.semaphore_signal(
            barrier, inc=1, device_id={"lat": lax.rem(me + d, n)}, device_id_type=MESH
        )

    every(greet)

    def rows_forward(w, ready):
        re, im = [], []
        for q in range(RADIX):
            cut = pl.ds(q * SUB, SUB)
            re.append(jnp.concatenate([src_ref[w, 0, :, cut], rec_ref[w, 0, :, cut]], axis=0))
            im.append(jnp.concatenate([src_ref[w, 1, :, cut], rec_ref[w, 1, :, cut]], axis=0))
        re, im = forward_four(re, im)
        for r in range(RADIX):
            pair = split(jnp.concatenate([re[r], im[r]], axis=0))
            with_cos = table_right(tab_ref, 1, r, 0, pair)
            with_sin = table_right(tab_ref, 1, r, 1, pair)
            parts = (
                with_cos[:LANES] + with_sin[LANES:],
                with_cos[LANES:] - with_sin[:LANES],
            )
            for c in range(2):
                for b in range(2):
                    piece = parts[c][:, b * LANES : (b + 1) * LANES]
                    low, high = halves(piece[:ROWS], piece[ROWS:], low_half)
                    peer = RADIX * r + 2 * b
                    send_f[w, peer, c] = low
                    send_f[w, peer + 1, c] = high
            if w == 0 and r == 0:
                ready()
            start_f(w, r)

    def make_shift(w, slot, j):
        speed = omega_ref[w] * slow_ref[j]
        vertical = speed * speed
        wide = lax.broadcasted_iota(jnp.int32, (ROWS, LANES), 1)
        tall = lax.broadcasted_iota(jnp.int32, (ROWS, LANES), 0)
        place = ROWS * (GROUPS * (base + slot) + along) + lax.rem(wide, ROWS)
        ky = signed_wave(place // SUB + RADIX * lax.rem(place, SUB))
        ky2 = ky * ky
        sign = jnp.where(wide < ROWS, -1.0, 1.0)
        scale = 1.0 / (POINTS * POINTS)

        @pl.loop(0, PEERS)
        def _(block):
            at = ROWS * block
            r = at // SUB
            kx = signed_wave(r + RADIX * (lax.rem(at, SUB) + tall))
            real, imag = shift_pair(vertical - (kx * kx + ky2))
            rows = pl.ds(pl.multiple_of(ROWS * block, ROWS), ROWS)
            shift[j, 0, rows, :] = real * scale
            shift[j, 1, rows, :] = imag * (sign * scale)

    def columns_forward(w, slot):
        re, im = [], []
        for q in range(RADIX):
            re.append(recv_f[w, slot, 4 * q : 4 * q + 4, 0].reshape(SUB, LANES))
            im.append(recv_f[w, slot, 4 * q : 4 * q + 4, 1].reshape(SUB, LANES))
        re, im = forward_four(re, im)
        for r in range(RADIX):
            pair = split(jnp.concatenate([re[r], im[r]], axis=1))
            with_cos = table_left(tab_ref, 0, r, 0, pair)
            with_sin = table_left(tab_ref, 0, r, 1, pair)
            spec[r, 0] = with_cos[:, :LANES] + with_sin[:, LANES:]
            spec[r, 1] = with_cos[:, LANES:] - with_sin[:, :LANES]

    def columns_backward(w, slot, j):
        re, im = [], []
        for r in range(RADIX):
            cos_shift = shift[j, 0, pl.ds(r * SUB, SUB), :]
            sin_shift = shift[j, 1, pl.ds(r * SUB, SUB), :]
            new_re = spec[r, 0] * cos_shift - spec[r, 1] * sin_shift
            new_im = spec[r, 0] * sin_shift + spec[r, 1] * cos_shift
            pair = split(jnp.concatenate([new_re, new_im], axis=1))
            with_cos = table_left(tab_ref, 1, r, 0, pair)
            with_sin = table_left(tab_ref, 1, r, 1, pair)
            re.append(with_cos[:, :LANES] - with_sin[:, LANES:])
            im.append(with_cos[:, LANES:] + with_sin[:, :LANES])
        flip = (1 - 2 * half).astype(jnp.float32)
        first = [a + b + flip * (c + d) for a, b, c, d in (
            (re[0], re[2], re[1], re[3]), (im[0], im[2], im[1], im[3]))]
        second = [
            re[0] - re[2] - flip * (im[1] - im[3]),
            im[0] - im[2] + flip * (re[1] - re[3]),
        ]
        for c in range(2):
            send_b[w, slot, j, 0:4, c] = first[c].reshape(4, ROWS, LANES)
            send_b[w, slot, j, 4:8, c] = second[c].reshape(4, ROWS, LANES)

    def rows_backward(w, j):
        re, im = [], []
        for r in range(RADIX):
            stacked = []
            for c in range(2):
                sides = [
                    halves(recv_b[w, j, 4 * r + 2 * b, c], recv_b[w, j, 4 * r + 2 * b + 1, c], low_half)
                    for b in range(2)
                ]
                for field in range(2):
                    stacked.append(jnp.concatenate([sides[0][field], sides[1][field]], axis=1))
            pair = split(jnp.concatenate(stacked, axis=0))
            with_cos = table_right(tab_ref, 0, r, 0, pair)
            with_sin = table_right(tab_ref, 0, r, 1, pair)
            re.append(with_cos[:LANES] - with_sin[LANES:])
            im.append(with_cos[LANES:] + with_sin[:LANES])
        parts = backward_four(re, im)
        for q in range(RADIX):
            cut = pl.ds(q * SUB, SUB)
            weight = index_ref[:, cut].astype(jnp.float32) / (INTERP - 1)
            for c in range(2):
                for field in range(2):
                    value = parts[c][q][ROWS * field : ROWS * (field + 1)]
                    if j == 0:
                        first_ref[field, c, :, cut] = (1.0 - weight) * value
                    else:
                        mixed = first_ref[field, c, :, cut] + weight * value
                        for b in range(2):
                            out_ref[w, field, c, 2 * q + b, pl.ds(HMAX, ROWS), :] = (
                                mixed[:, b * LANES : (b + 1) * LANES]
                            )

    @pl.when(me == 0)
    def _():
        for w in range(2):
            out_ref[w, :, :, :, pl.ds(0, HMAX), :] = jnp.zeros((2, 2, BANDS, HMAX, LANES), jnp.float32)

    @pl.when(me == n - 1)
    def _():
        for w in range(2):
            out_ref[w, :, :, :, pl.ds(HMAX + ROWS, HMAX), :] = jnp.zeros((2, 2, BANDS, HMAX, LANES), jnp.float32)

    rows_forward(0, lambda: pl.semaphore_wait(barrier, n - 1))
    rows_forward(1, None)

    @pl.loop(0, 2 * slots)
    def _(chunk):
        w = jnp.where(chunk < slots, 0, 1)
        slot = chunk - slots * w
        for j in range(2):
            make_shift(w, slot, j)
        wait_f(w, slot)
        columns_forward(w, slot)
        for j in range(2):
            columns_backward(w, slot, j)
            start_b(w, slot, j)

    for w in range(2):
        for j in range(2):
            wait_b(w, j)
            rows_backward(w, j)

        @pl.when(me < n - 1)
        def _():
            halo(w, 0).start()

        @pl.when(me > 0)
        def _():
            halo(w, 1).start()

    for w in range(2):
        for group in range(GROUPS):
            each_f(w, group, lambda copy: copy.wait_send())

        @pl.loop(0, slots)
        def _(slot):
            for j in range(2):
                each_b(w, slot, j, lambda copy: copy.wait_send())

        @pl.when(me < n - 1)
        def _():
            halo(w, 0).wait_send()
            halo(w, 1).wait_recv()

        @pl.when(me > 0)
        def _():
            halo(w, 1).wait_send()
            halo(w, 0).wait_recv()


def image_kernel(lags_ref, fields_ref, out_ref):
    lag = lags_ref[pl.program_id(0)]
    for band in range(BANDS):
        total = None
        for w in range(2):
            for c in range(2):
                source = fields_ref[w, 0, c, band, pl.ds(HMAX - lag, ROWS), :]
                receiver = fields_ref[w, 1, c, band, pl.ds(HMAX + lag, ROWS), :]
                term = source * receiver
                total = term if total is None else total + term
        out_ref[0, :, pl.ds(band * LANES, LANES)] = total


def fused(source_field, receiver_field, ref_slowness, omega, interp_index, lags):
    tables = jnp.asarray(fourier_tables())
    vmem = pl.BlockSpec(memory_space=pltpu.VMEM)
    smem = pl.BlockSpec(memory_space=pltpu.SMEM)
    f32 = jnp.float32
    block = (PEERS, 2, ROWS, LANES)
    dma = pltpu.SemaphoreType.DMA
    migrated = pl.pallas_call(
        migrate_kernel,
        out_shape=jax.ShapeDtypeStruct((2, 2, 2, BANDS, ROWS + 2 * HMAX, LANES), f32),
        in_specs=[smem, smem, vmem, vmem, vmem, vmem],
        out_specs=vmem,
        scratch_shapes=[
            pltpu.VMEM((2,) + block, f32),
            pltpu.VMEM((2, SLOTS) + block, f32),
            pltpu.VMEM((2, SLOTS, 2, HALF) + block[1:], f32),
            pltpu.VMEM((2, 2) + block, f32),
            pltpu.VMEM((RADIX, 2, SUB, LANES), f32),
            pltpu.VMEM((2, 2, POINTS, LANES), f32),
            pltpu.VMEM((2, 2, ROWS, POINTS), f32),
            dma((2, PEERS, 2)), dma((2, SLOTS, PEERS)),
            dma((2, SLOTS, 2, HALF)), dma((2, 2, PEERS)),
            dma((2, 2)), dma((2, 2)),
        ],
        compiler_params=pltpu.CompilerParams(
            collective_id=0, has_side_effects=True, vmem_limit_bytes=40 * 2**20
        ),
    )(omega, ref_slowness, source_field, receiver_field, interp_index, tables)
    count = lags.shape[0]
    return pl.pallas_call(
        image_kernel,
        grid_spec=pltpu.PrefetchScalarGridSpec(
            num_scalar_prefetch=1,
            grid=(count,),
            in_specs=[pl.BlockSpec(migrated.shape, lambda i, lags: (0,) * 6)],
            out_specs=pl.BlockSpec((1, ROWS, POINTS), lambda i, lags: (i, 0, 0)),
        ),
        out_shape=jax.ShapeDtypeStruct((count, ROWS, POINTS), f32),
        compiler_params=pltpu.CompilerParams(vmem_limit_bytes=24 * 2**20),
    )(lags, migrated)


def body(source_field, receiver_field, ref_slowness, omega, interp_index, lags):
    args = (source_field, receiver_field, ref_slowness, omega, interp_index, lags)
    fits = source_field.shape == (2, 2, ROWS, POINTS) and lax.axis_size("lat") == PEERS
    return fused(*args) if fits else local(*args)


def solution(mesh):
    in_specs = (
        P("shots", None, "lat", None),
        P("shots", None, "lat", None),
        P(),
        P(),
        P("lat", None),
        P(),
    )
    out_specs = P("shots", "lat", None)
    return jax.shard_map(body, mesh=mesh, in_specs=in_specs, out_specs=out_specs, check_vma=False)
```
